256 devices in a mesh: ex: 32 (over z, y_lo, core), feat: 8 (over y_hi, x).
Axes of the slice: x: 4, y: 4 (y_hi: 2, y_lo: 2; y = y_hi * 2 + y_lo), z: 8, core: 2. Of those that a mesh axis runs over, the one named last changes fastest.
Arguments:
- grads: bfloat16 [8192, 8192], P('ex', 'feat'), may hold values from -6 to 6
- lr_plan: float32 [64], replicated, may hold values from 0.1 to 1
- ckpt_step: int32 [4], replicated, may hold values from 0 to 63
Outputs:
- influence: float32 [8192, 8192], P('ex', 'feat')
The draws below stay inside these ranges and needn't reach their ends.
All inputs are finite; a program needn't handle non-finite values.
Results may differ from the reference program's by a relative error of at most 0.003.
Values may be sent and summed in bfloat16 or wider, within the bound.
No kernel may reach another device: no remote copies, remote signals or barrier semaphores. Data moves between devices by JAX's collectives and lax.ppermute only.
A program may use at most 64 MiB of HBM per device.

```python
import math
import jax
import jax.numpy as jnp

PROJ = 2048
CKPT = 4
SCHED = 64
EXAMPLES = 8192
FEATURES = 8192


def place_ends(drawn, key, least, largest):
    longest = drawn.shape.index(max(drawn.shape))
    spots = []
    for shift in (0, 1):
        where = [jax.random.randint(jax.random.fold_in(key, axis), (), 0, length) for axis, length in enumerate(drawn.shape)]
        where[longest] = (where[longest] + shift) % drawn.shape[longest]
        spots.append(tuple(where))
    return drawn.at[spots[0]].set(least).at[spots[1]].set(largest)


def steps_of(rng, shape, split, least, largest):
    loudness = 1.0
    for axis_at, parts in split:
        heights = jax.random.uniform(jax.random.fold_in(jax.random.fold_in(rng, 6), axis_at), (parts,), jnp.float32, least / len(split), largest / len(split))
        loudness = loudness * jnp.repeat(jnp.exp(heights), shape[axis_at] // parts).reshape((-1,) + (1,) * (len(shape) - 1 - axis_at))
    return loudness


def bell_draw(stream_key, shape, deviation, limit, cuts=(), held_as=jnp.bfloat16):
    level = steps_of(stream_key, shape, cuts, -0.22, 0.18) if cuts else 1.0
    values = jax.random.normal(stream_key, shape, jnp.float32) * deviation * level
    return jnp.minimum(jnp.maximum(values, -limit), limit).astype(held_as)


def setup_inputs(seed: int = 0) -> dict:
    key_list = jax.random.split(jax.random.key(seed), 4)
    grads = bell_draw(key_list[0], (EXAMPLES, FEATURES), 1.0, 6.0, ((0, 32), (1, 8)))
    lr_plan = jnp.clip(jnp.exp(jax.random.uniform(key_list[1], (SCHED,), jnp.float32, math.log(0.1), math.log(1.0))), 0.1, 1.0)
    ckpt_step = place_ends(jax.random.randint(key_list[2], (CKPT,), 0, SCHED), jax.random.fold_in(key_list[2], 1), 0, SCHED - 1).astype(jnp.int32)
    return {"grads": grads, "lr_plan": lr_plan, "ckpt_step": ckpt_step}


def reference(grads, lr_plan, ckpt_step):
    rate = lr_plan[ckpt_step.astype(jnp.int32)]
    weight = rate / jnp.sum(rate) * (CKPT / jnp.sqrt(jnp.float32(FEATURES)))
    column_weight = jnp.repeat(weight, PROJ)
    scaled = (grads.astype(jnp.float32) * jnp.sqrt(column_weight)[None, :]).astype(jnp.bfloat16)
    return jnp.dot(scaled, scaled.T, preferred_element_type=jnp.float32)
```

```python
import jax
import jax.numpy as jnp
from jax import lax
from jax.experimental import pallas as pl
from jax.experimental.pallas import tpu as pltpu
from jax.sharding import Mesh, PartitionSpec as P

PROJ = 2048
CKPT = 4
FEATURES = 8192

Z, YL, C, YH, X = "z", "ylo", "core", "yhi", "x"
NZ, NX = 8, 4
SMEM = pl.BlockSpec(memory_space=pltpu.SMEM)
VMEM = pl.BlockSpec(memory_space=pltpu.VMEM)
HBM = pl.BlockSpec(memory_space=pltpu.HBM)


def take_from(value, axis, size, step):
    return lax.ppermute(value, axis, [(i, (i - step) % size) for i in range(size)])


def dot_t(left, right):
    return lax.dot_general(left, right, (((1,), (1,)), ((), ())), preferred_element_type=jnp.float32)


def scale_kernel(plan_ref, step_ref, grads_ref, out_ref, *quarter_refs):
    x = lax.axis_index(X)
    mine = ((lax.axis_index(YH) * NX + x) * grads_ref.shape[1]) // PROJ
    rate = [plan_ref[step_ref[i]] for i in range(CKPT)]
    own = plan_ref[step_ref[mine]]
    whole = rate[0] + rate[1] + rate[2] + rate[3]
    shape = (8, grads_ref.shape[1])
    weight = jnp.full(shape, own, jnp.float32) / jnp.full(shape, whole, jnp.float32)
    weight = weight * (CKPT / jnp.sqrt(jnp.full(shape, FEATURES, jnp.float32)))
    factor = jnp.sqrt(weight)[:1]
    out_ref[...] = (grads_ref[...].astype(jnp.float32) * factor).astype(jnp.bfloat16)
    for ref, dx in zip(quarter_refs, (0, 1, -1, 2)):
        q = ref.shape[0]
        first = pl.multiple_of(((x - dx + NX) % NX) * q, q)
        ref[...] = out_ref[pl.ds(first, q), :]


def scale(grads, lr_plan, ckpt_step):
    rows, width = grads.shape
    quarter = jax.ShapeDtypeStruct((rows // NX, width), jnp.bfloat16)
    return pl.pallas_call(
        scale_kernel,
        out_shape=[jax.ShapeDtypeStruct((rows, width), jnp.bfloat16)] + [quarter] * NX,
        in_specs=[SMEM, SMEM, VMEM],
        out_specs=[VMEM] * (1 + NX),
        name="scale",
    )(lr_plan, ckpt_step, grads)


def early_products(lefts, rights):
    rows, width = rights[0][0].shape
    q, nd, nk = rows // NX, len(lefts), len(rights[0])
    pieces = [r for block in rights for r in block]

    def kernel(*refs):
        left_in, right_in = refs[:nd], refs[nd : nd + len(pieces)]
        right, acc, left, lsem, rsem = refs[nd + len(pieces) :]
        lcopies = [pltpu.make_async_copy(left_in[i], left.at[i], lsem.at[i]) for i in range(nd)]
        rcopies = [
            pltpu.make_async_copy(
                right_in[i], right.at[i // nk, :, pl.ds(i % nk * width, width)], rsem.at[i]
            )
            for i in range(len(pieces))
        ]
        for copy in lcopies + rcopies:
            copy.start()
        for copy in lcopies:
            copy.wait()
        for block in range(4):
            total = 0.0
            for k in range(nk):
                rcopies[block * nk + k].wait()
                part = left[:, k * q : (k + 1) * q, :].reshape(nd * q, width)
                total = total + dot_t(part, right[block, :, k * width : (k + 1) * width])
            acc[block] = total

    return pl.pallas_call(
        kernel,
        out_shape=[
            jax.ShapeDtypeStruct((4, rows, nk * width), jnp.bfloat16),
            jax.ShapeDtypeStruct((4, nd * q, rows), jnp.float32),
        ],
        in_specs=[HBM] * (nd + len(pieces)),
        out_specs=[VMEM, VMEM],
        scratch_shapes=[
            pltpu.VMEM((nd, rows, width), jnp.bfloat16),
            pltpu.SemaphoreType.DMA((nd,)),
            pltpu.SemaphoreType.DMA((len(pieces),)),
        ],
        compiler_params=pltpu.CompilerParams(vmem_limit_bytes=32 * 2**20),
        cost_estimate=pl.CostEstimate(
            flops=2 * nd * q * 4 * rows * nk * width,
            bytes_accessed=2 * (nd + len(pieces)) * rows * width,
            transcendentals=0,
        ),
        name="early",
    )(*lefts, *pieces)


def late_products(right, acc, early, late, far, ds):
    rows, width = far[0].shape
    q, ne, nl = rows // NX, len(early), len(late)
    nk = NX - 1

    def kernel(right, acc, *refs):
        late_in, early_in, far_in = refs[:nl], refs[nl : nl + ne], refs[nl + ne : nl + ne + 4]
        out, left, tail, block_in, sums, sem = refs[nl + ne + 4 :]
        z, a, c = (lax.axis_index(n) for n in (Z, YL, C))
        moves = [(late_in[i], left.at[i]) for i in range(nl)]
        moves += [
            (early_in[i].at[pl.ds(nk * q, q)], tail.at[pl.ds(i * q, q)]) for i in range(ne)
        ]
        moves += [(far_in[i], block_in.at[i]) for i in range(4)]
        copies = [pltpu.make_async_copy(a, b, sem.at[i]) for i, (a, b) in enumerate(moves)]
        for copy in copies:
            copy.start()
        for copy in copies[:nl]:
            copy.wait()

        def part(k):
            return left[:, k * q : (k + 1) * q, :].reshape(nl * q, width)

        for block in range(4):
            total = 0.0
            for k in range(nk):
                total = total + dot_t(part(k), right[block, :, k * width : (k + 1) * width])
            sums[block] = total
        for copy in copies[nl:]:
            copy.wait()
        for block in range(4):
            ylo, core = (a + block // 2) % 2, (c + block % 2) % 2
            base = (ylo * 2 + core) * NZ
            first = (acc[block] + dot_t(tail[...], block_in[block])).astype(jnp.bfloat16)
            second = (sums[block] + dot_t(part(nk), block_in[block])).astype(jnp.bfloat16)
            for i, d in enumerate(ds):
                tile = first[i * q : (i + 1) * q] if i < ne else second[(i - ne) * q : (i - ne + 1) * q]
                out[base + (z + d + NZ) % NZ] = tile

    n_moves = 4 + ne + nl
    return pl.pallas_call(
        kernel,
        out_shape=jax.ShapeDtypeStruct((4 * NZ, q, rows), jnp.bfloat16),
        in_specs=[VMEM, VMEM] + [HBM] * n_moves,
        out_specs=VMEM,
        scratch_shapes=[
            pltpu.VMEM((nl, rows, width), jnp.bfloat16),
            pltpu.VMEM((ne * q, width), jnp.bfloat16),
            pltpu.VMEM((4, rows, width), jnp.bfloat16),
            pltpu.VMEM((4, nl * q, rows), jnp.float32),
            pltpu.SemaphoreType.DMA((n_moves,)),
        ],
        compiler_params=pltpu.CompilerParams(vmem_limit_bytes=32 * 2**20),
        cost_estimate=pl.CostEstimate(
            flops=2 * (nl * NX + ne) * q * 4 * rows * width,
            bytes_accessed=2 * n_moves * rows * width,
            transcendentals=0,
        ),
        name="late",
    )(right, acc, *late, *early, *far)


def after(values, done):
    return lax.optimization_barrier((tuple(values), tuple(done)))[0]


def on_device(grads, lr_plan, ckpt_step):
    c = lax.axis_index(C)
    s, *quarters = scale(grads, lr_plan, ckpt_step)
    rows = s.shape[0]
    swap = lambda v: take_from(v, C, 2, 1)

    heads = [take_from(v, X, NX, dx) for v, dx in zip(quarters[1:], (1, -1, 2))]
    other = take_from(s, YL, 2, 1)
    ring = {0: jnp.concatenate([quarters[0]] + heads, axis=0)}
    ring[1], ring[-1] = take_from(ring[0], Z, NZ, 1), take_from(ring[0], Z, NZ, -1)
    (ready,) = after((s,), heads)
    fs, bs = take_from(ready, X, NX, 1), take_from(ready, X, NX, -1)

    up, down = after((ring[1], ring[-1]), (fs, bs))
    ring[2], ring[-2] = take_from(up, Z, NZ, 1), take_from(down, Z, NZ, -1)
    (ready,) = after((other,), (fs, bs))
    fo, bo = take_from(ready, X, NX, 1), take_from(ready, X, NX, -1)

    up, down = after((ring[2], ring[-2]), (fo, bo))
    ring[3], ring[-3] = take_from(up, Z, NZ, 1), take_from(down, Z, NZ, -1)
    f_ready, b_ready = after((fs, bo), (fo, bo))
    far_s, far_o = take_from(f_ready, X, NX, 1), take_from(b_ready, X, NX, -1)

    ends = jnp.where(c == 0, ring[3], ring[-3])
    pairs = [((i + 1) % NZ * 2, i * 2) for i in range(NZ)]
    pairs += [(i * 2 + 1, (i + 1) % NZ * 2 + 1) for i in range(NZ)]
    ring[4] = lax.ppermute(ends, (Z, C), pairs)

    s_ready, o_ready = after((s, other), (fs, bs))
    far_s_ready, far_o_ready = after((far_s, far_o), (ring[3], ring[-3]))
    own = [[s, fs, bs], [other, fo, bo]]
    rights = [own[0], [swap(v) for v in (s_ready, fs, bs)], own[1], [swap(v) for v in (o_ready, fo, bo)]]
    far = [far_s, swap(far_s_ready), far_o, swap(far_o_ready)]

    first = [ring[d] for d in (0, 1, -1, 2, -2)]
    right, acc = early_products(first, rights)
    send = late_products(
        right, acc, first, [ring[3], ring[-3], ring[4]], far, (0, 1, -1, 2, -2, 3, -3, 4)
    )
    got = lax.all_to_all(send, (YL, C, YH, X), 0, 0)
    q = rows // NX
    got = got.reshape(2, 2, 2, NX, q, rows).astype(jnp.float32)
    total = got[:, :, 0] + got[:, :, 1]
    return total.reshape(2 * 2 * NX * q, rows).T


def solution(mesh):
    fine = Mesh(mesh.devices.reshape(NZ, 2, 2, 2, NX), (Z, YL, C, YH, X))
    spec = P((Z, YL, C), (YH, X))
    return jax.shard_map(
        on_device, mesh=fine, in_specs=(spec, P(), P()), out_specs=spec, check_vma=False
    )
```

```python
import jax
import jax.numpy as jnp
from jax import lax
from jax.experimental import pallas as pl
from jax.experimental.pallas import tpu as pltpu
from jax.sharding import Mesh, PartitionSpec as P

PROJ = 2048
CKPT = 4
FEATURES = 8192

Z, YL, C, YH, X = "z", "ylo", "core", "yhi", "x"
NZ, NX = 8, 4
SMEM = pl.BlockSpec(memory_space=pltpu.SMEM)
VMEM = pl.BlockSpec(memory_space=pltpu.VMEM)
HBM = pl.BlockSpec(memory_space=pltpu.HBM)


def take_from(value, axis, size, step):
    return lax.ppermute(value, axis, [(i, (i - step) % size) for i in range(size)])


def dot_t(left, right):
    return lax.dot_general(left, right, (((1,), (1,)), ((), ())), preferred_element_type=jnp.float32)


def scale_kernel(plan_ref, step_ref, grads_ref, out_ref, *quarter_refs):
    x = lax.axis_index(X)
    mine = ((lax.axis_index(YH) * NX + x) * grads_ref.shape[1]) // PROJ
    rate = [plan_ref[step_ref[i]] for i in range(CKPT)]
    own = plan_ref[step_ref[mine]]
    whole = rate[0] + rate[1] + rate[2] + rate[3]
    shape = (8, grads_ref.shape[1])
    weight = jnp.full(shape, own, jnp.float32) / jnp.full(shape, whole, jnp.float32)
    weight = weight * (CKPT / jnp.sqrt(jnp.full(shape, FEATURES, jnp.float32)))
    factor = jnp.sqrt(weight)[:1]
    out_ref[...] = (grads_ref[...].astype(jnp.float32) * factor).astype(jnp.bfloat16)
    for ref, dx in zip(quarter_refs, (0, 1, -1, 2)):
        q = ref.shape[0]
        first = pl.multiple_of(((x - dx + NX) % NX) * q, q)
        ref[...] = out_ref[pl.ds(first, q), :]


def scale(grads, lr_plan, ckpt_step):
    rows, width = grads.shape
    quarter = jax.ShapeDtypeStruct((rows // NX, width), jnp.bfloat16)
    return pl.pallas_call(
        scale_kernel,
        out_shape=[jax.ShapeDtypeStruct((rows, width), jnp.bfloat16)] + [quarter] * NX,
        in_specs=[SMEM, SMEM, VMEM],
        out_specs=[VMEM] * (1 + NX),
        name="scale",
    )(lr_plan, ckpt_step, grads)


def copy_all(moves, sem):
    copies = [pltpu.make_async_copy(src, dst, sem.at[i]) for i, (src, dst) in enumerate(moves)]
    for copy in copies:
        copy.start()
    return copies


def cost(flops, bytes_accessed):
    return pl.CostEstimate(flops=flops, bytes_accessed=bytes_accessed, transcendentals=0)


def vmem_out(*shape, dtype=jnp.bfloat16):
    return jax.ShapeDtypeStruct(shape, dtype)


PARAMS = pltpu.CompilerParams(vmem_limit_bytes=16 * 2**20)


def own_products(lefts, rights):
    rows, width = lefts[0].shape
    q, nd, nk = rows // NX, len(lefts), len(rights[0])

    def kernel(*refs):
        left_in, right_in = refs[:nd], refs[nd : nd + 2 * nk]
        left, right, acc, sem = refs[nd + 2 * nk :]
        moves = [(left_in[i], left.at[i]) for i in range(nd)]
        moves += [
            (right_in[i], right.at[i // nk, :, pl.ds(i % nk * width, width)]) for i in range(2 * nk)
        ]
        copies = copy_all(moves, sem)
        for copy in copies[:nd]:
            copy.wait()
        for half in range(2):
            total = 0.0
            for k in range(nk):
                copies[nd + half * nk + k].wait()
                part = left[:, k * q : (k + 1) * q, :].reshape(nd * q, width)
                total = total + dot_t(part, right[half, :, k * width : (k + 1) * width])
            acc[half] = total

    return pl.pallas_call(
        kernel,
        out_shape=[
            vmem_out(nd, rows, width),
            vmem_out(2, rows, nk * width),
            vmem_out(2, nd * q, rows, dtype=jnp.float32),
        ],
        in_specs=[HBM] * (nd + 2 * nk),
        out_specs=[VMEM] * 3,
        scratch_shapes=[pltpu.SemaphoreType.DMA((nd + 2 * nk,))],
        compiler_params=PARAMS,
        cost_estimate=cost(4 * nd * q * rows * nk * width, 2 * (nd + 2 * nk) * rows * width),
        name="own",
    )(*lefts, *rights[0], *rights[1])


def all_products(left, acc, rights, fars):
    nd, rows, width = left.shape
    q, nk = rows // NX, len(rights[0])

    def kernel(left, acc, *refs):
        right_in, far_in = refs[: 2 * nk], refs[2 * nk : 2 * nk + 2]
        right, far, out, sem = refs[2 * nk + 2 :]
        moves = [
            (right_in[i], right.at[i // nk, :, pl.ds(i % nk * width, width)]) for i in range(2 * nk)
        ]
        moves += [(far_in[i], far.at[i]) for i in range(2)]
        copies = copy_all(moves, sem)

        def part(k):
            return left[:, k * q : (k + 1) * q, :].reshape(nd * q, width)

        for half in range(2):
            total = 0.0
            for k in range(nk):
                copies[half * nk + k].wait()
                total = total + dot_t(part(k), right[half, :, k * width : (k + 1) * width])
            out[2 * half + 1] = total.astype(jnp.bfloat16).reshape(nd, q, rows)
        for half in range(2):
            copies[2 * nk + half].wait()
            total = acc[half] + dot_t(part(nk - 1), far[half])
            out[2 * half] = total.astype(jnp.bfloat16).reshape(nd, q, rows)

    return pl.pallas_call(
        kernel,
        out_shape=[
            vmem_out(2, rows, nk * width),
            vmem_out(2, rows, width),
            vmem_out(4, nd, q, rows),
        ],
        in_specs=[VMEM, VMEM] + [HBM] * (2 * nk + 2),
        out_specs=[VMEM] * 3,
        scratch_shapes=[pltpu.SemaphoreType.DMA((2 * nk + 2,))],
        compiler_params=PARAMS,
        cost_estimate=cost(4 * nd * q * rows * (nk + 1) * width, 4 * (nk + 1) * rows * width),
        name="rest",
    )(left, acc, *rights[0], *rights[1], *fars)


def late_products(done, right_own, far_own, right_other, lefts, last, ds):
    nd, q, rows = done.shape[1:]
    width = far_own.shape[2]
    nl, half_rows, nk = len(lefts) + 1, rows // 2, NX

    def kernel(done, right_own, far_own, right_other, *refs):
        left_in, out, left, sem = refs[: nl + 1], refs[-3], refs[-2], refs[-1]
        z, a, c = (lax.axis_index(n) for n in (Z, YL, C))
        moves = [(left_in[i], left.at[i]) for i in range(nl - 1)]
        moves += [
            (left_in[nl - 1 + i], left.at[nl - 1, pl.ds(i * half_rows, half_rows)]) for i in range(2)
        ]
        copies = copy_all(moves, sem)

        def place(block, d):
            ylo, core = (a + block // 2) % 2, (c + block % 2) % 2
            return (ylo * 2 + core) * NZ + (z + d + NZ) % NZ

        for block in range(4):
            for i in range(nd):
                out[place(block, ds[i])] = done[block, i]
        for copy in copies:
            copy.wait()
        for block in range(4):
            half, total = block // 2, 0.0
            for k in range(nk):
                columns = slice(k * width, (k + 1) * width)
                if block % 2:
                    right = right_other[half, :, columns]
                else:
                    right = right_own[half, :, columns] if k < nk - 1 else far_own[half]
                total = total + dot_t(left[:, k * q : (k + 1) * q, :].reshape(nl * q, width), right)
            total = total.astype(jnp.bfloat16)
            for i in range(nl):
                out[place(block, ds[nd + i])] = total[i * q : (i + 1) * q]

    return pl.pallas_call(
        kernel,
        out_shape=vmem_out(4 * NZ, q, rows),
        in_specs=[VMEM] * 4 + [HBM] * (nl + 1),
        out_specs=VMEM,
        scratch_shapes=[
            pltpu.VMEM((nl, rows, width), jnp.bfloat16),
            pltpu.SemaphoreType.DMA((nl + 1,)),
        ],
        compiler_params=PARAMS,
        cost_estimate=cost(8 * nl * q * rows * nk * width, 2 * nl * rows * width),
        name="late",
    )(done, right_own, far_own, right_other, *lefts, *last)


def after(values, done):
    return lax.optimization_barrier((tuple(values), tuple(done)))[0]


def on_device(grads, lr_plan, ckpt_step):
    s, *quarters = scale(grads, lr_plan, ckpt_step)
    rows = s.shape[0]
    swap = lambda v: take_from(v, C, 2, 1)

    heads = [take_from(v, X, NX, dx) for v, dx in zip(quarters[1:], (1, -1, 2))]
    other = take_from(s, YL, 2, 1)
    ring = {0: jnp.concatenate([quarters[0]] + heads, axis=0)}
    ring[1], ring[-1] = take_from(ring[0], Z, NZ, 1), take_from(ring[0], Z, NZ, -1)
    (ready,) = after((s,), heads)
    fs, bs = take_from(ready, X, NX, 1), take_from(ready, X, NX, -1)

    (up,), (down,) = after((ring[1],), (fs,)), after((ring[-1],), (bs,))
    ring[2], ring[-2] = take_from(up, Z, NZ, 1), take_from(down, Z, NZ, -1)
    (f_ready,), (b_ready,) = after((other,), (fs,)), after((other,), (bs,))
    fo, bo = take_from(f_ready, X, NX, 1), take_from(b_ready, X, NX, -1)

    (up,), (down,) = after((ring[2],), (fo,)), after((ring[-2],), (bo,))
    ring[3], ring[-3] = take_from(up, Z, NZ, 1), take_from(down, Z, NZ, -1)
    (f_ready,), (b_ready,) = after((fs,), (fo,)), (bo,)
    far_s, far_o = take_from(f_ready, X, NX, 1), take_from(b_ready, X, NX, -1)

    first = [ring[d] for d in (0, 1, -1, 2, -2)]
    left, right_own, acc = own_products(first, [[s, fs, bs], [other, fo, bo]])
    half = rows // 2
    (down,) = (ring[-3],)
    last = (take_from(ring[3][:half], Z, NZ, 1), take_from(down[half:], Z, NZ, -1))

    ready = after((s, fs, bs, other), (fs, bs))
    ready += after((fo, bo, far_s, far_o), (ring[3], ring[-3]))
    swapped = [swap(v) for v in ready]
    right_other, far_own, done = all_products(
        left,
        acc,
        [swapped[:3] + swapped[6:7], swapped[3:6] + swapped[7:]],
        [far_s, far_o],
    )
    send = late_products(
        done, right_own, far_own, right_other, [ring[3], ring[-3]], last, (0, 1, -1, 2, -2, 3, -3, 4)
    )
    got = lax.all_to_all(send, (YL, C, YH, X), 0, 0)
    q = rows // NX
    got = got.reshape(2, 2, 2, NX, q, rows).astype(jnp.float32)
    total = got[:, :, 0] + got[:, :, 1]
    return total.reshape(2 * 2 * NX * q, rows).T


def solution(mesh):
    fine = Mesh(mesh.devices.reshape(NZ, 2, 2, 2, NX), (Z, YL, C, YH, X))
    spec = P((Z, YL, C), (YH, X))
    return jax.shard_map(
        on_device, mesh=fine, in_specs=(spec, P(), P()), out_specs=spec, check_vma=False
    )
```

```python
import jax
import jax.numpy as jnp
from jax import lax
from jax.experimental import pallas as pl
from jax.experimental.pallas import tpu as pltpu
from jax.sharding import Mesh, PartitionSpec as P

PROJ = 2048
CKPT = 4
FEATURES = 8192

Z, YL, C, YH, X = "z", "ylo", "core", "yhi", "x"
NZ, NX = 8, 4
SMEM = pl.BlockSpec(memory_space=pltpu.SMEM)
VMEM = pl.BlockSpec(memory_space=pltpu.VMEM)
HBM = pl.BlockSpec(memory_space=pltpu.HBM)


def take_from(value, axis, size, step):
    return lax.ppermute(value, axis, [(i, (i - step) % size) for i in range(size)])


def dot_t(left, right):
    return lax.dot_general(left, right, (((1,), (1,)), ((), ())), preferred_element_type=jnp.float32)


def scale_kernel(plan_ref, step_ref, grads_ref, out_ref, *quarter_refs):
    x = lax.axis_index(X)
    mine = ((lax.axis_index(YH) * NX + x) * grads_ref.shape[1]) // PROJ
    rate = [plan_ref[step_ref[i]] for i in range(CKPT)]
    own = plan_ref[step_ref[mine]]
    whole = rate[0] + rate[1] + rate[2] + rate[3]
    shape = (8, grads_ref.shape[1])
    weight = jnp.full(shape, own, jnp.float32) / jnp.full(shape, whole, jnp.float32)
    weight = weight * (CKPT / jnp.sqrt(jnp.full(shape, FEATURES, jnp.float32)))
    factor = jnp.sqrt(weight)[:1]
    out_ref[...] = (grads_ref[...].astype(jnp.float32) * factor).astype(jnp.bfloat16)
    for ref, dx in zip(quarter_refs, (0, 1, -1, 2)):
        q = ref.shape[0]
        first = pl.multiple_of(((x - dx + NX) % NX) * q, q)
        ref[...] = out_ref[pl.ds(first, q), :]


def scale(grads, lr_plan, ckpt_step):
    rows, width = grads.shape
    quarter = jax.ShapeDtypeStruct((rows // NX, width), jnp.bfloat16)
    return pl.pallas_call(
        scale_kernel,
        out_shape=[jax.ShapeDtypeStruct((rows, width), jnp.bfloat16)] + [quarter] * NX,
        in_specs=[SMEM, SMEM, VMEM],
        out_specs=[VMEM] * (1 + NX),
        name="scale",
    )(lr_plan, ckpt_step, grads)


def copy_all(moves, sem):
    copies = [pltpu.make_async_copy(src, dst, sem.at[i]) for i, (src, dst) in enumerate(moves)]
    for copy in copies:
        copy.start()
    return copies


def cost(flops, bytes_accessed):
    return pl.CostEstimate(flops=flops, bytes_accessed=bytes_accessed, transcendentals=0)


def vmem_out(*shape, dtype=jnp.bfloat16):
    return jax.ShapeDtypeStruct(shape, dtype)


PARAMS = pltpu.CompilerParams(vmem_limit_bytes=16 * 2**20)


def own_products(lefts, rights):
    rows, width = lefts[0].shape
    q, nd, nk = rows // NX, len(lefts), len(rights[0])

    def kernel(*refs):
        left_in, right_in = refs[:nd], refs[nd : nd + 2 * nk]
        left, right, acc, sem = refs[nd + 2 * nk :]
        moves = [(left_in[i], left.at[i]) for i in range(nd)]
        moves += [
            (right_in[i], right.at[i // nk, :, pl.ds(i % nk * width, width)]) for i in range(2 * nk)
        ]
        copies = copy_all(moves, sem)
        for copy in copies[:nd]:
            copy.wait()
        for half in range(2):
            total = 0.0
            for k in range(nk):
                copies[nd + half * nk + k].wait()
                part = left[:, k * q : (k + 1) * q, :].reshape(nd * q, width)
                total = total + dot_t(part, right[half, :, k * width : (k + 1) * width])
            acc[half] = total

    return pl.pallas_call(
        kernel,
        out_shape=[
            vmem_out(nd, rows, width),
            vmem_out(2, rows, nk * width),
            vmem_out(2, nd * q, rows, dtype=jnp.float32),
        ],
        in_specs=[HBM] * (nd + 2 * nk),
        out_specs=[VMEM] * 3,
        scratch_shapes=[pltpu.SemaphoreType.DMA((nd + 2 * nk,))],
        compiler_params=PARAMS,
        cost_estimate=cost(4 * nd * q * rows * nk * width, 2 * (nd + 2 * nk) * rows * width),
        name="own",
    )(*lefts, *rights[0], *rights[1])


def all_products(left, acc, rights, fars):
    nd, rows, width = left.shape
    q, nk = rows // NX, len(rights[0])

    def kernel(left, acc, *refs):
        right_in, far_in = refs[: 2 * nk], refs[2 * nk : 2 * nk + 2]
        right, far, out, sem = refs[2 * nk + 2 :]
        moves = [
            (right_in[i], right.at[i // nk, :, pl.ds(i % nk * width, width)]) for i in range(2 * nk)
        ]
        moves += [(far_in[i], far.at[i]) for i in range(2)]
        copies = copy_all(moves, sem)

        def part(k):
            return left[:, k * q : (k + 1) * q, :].reshape(nd * q, width)

        for half in range(2):
            total = 0.0
            for k in range(nk):
                copies[half * nk + k].wait()
                total = total + dot_t(part(k), right[half, :, k * width : (k + 1) * width])
            out[2 * half + 1] = total.astype(jnp.bfloat16).reshape(nd, q, rows)
        for half in range(2):
            copies[2 * nk + half].wait()
            total = acc[half] + dot_t(part(nk - 1), far[half])
            out[2 * half] = total.astype(jnp.bfloat16).reshape(nd, q, rows)

    return pl.pallas_call(
        kernel,
        out_shape=[
            vmem_out(2, rows, nk * width),
            vmem_out(2, rows, width),
            vmem_out(4, nd, q, rows),
        ],
        in_specs=[VMEM, VMEM] + [HBM] * (2 * nk + 2),
        out_specs=[VMEM] * 3,
        scratch_shapes=[pltpu.SemaphoreType.DMA((2 * nk + 2,))],
        compiler_params=PARAMS,
        cost_estimate=cost(4 * nd * q * rows * (nk + 1) * width, 4 * (nk + 1) * rows * width),
        name="rest",
    )(left, acc, *rights[0], *rights[1], *fars)


def late_products(done, right_own, far_own, right_other, lefts, last, ds):
    nd, q, rows = done.shape[1:]
    width = far_own.shape[2]
    nl, half_rows, nk = len(lefts) + 1, rows // 2, NX

    def kernel(done, right_own, far_own, right_other, *refs):
        left_in, out, left, sem = refs[: nl + 1], refs[-3], refs[-2], refs[-1]
        z, a, c = (lax.axis_index(n) for n in (Z, YL, C))
        moves = [(left_in[i], left.at[i]) for i in range(nl - 1)]
        moves += [
            (left_in[nl - 1 + i], left.at[nl - 1, pl.ds(i * half_rows, half_rows)]) for i in range(2)
        ]
        copies = copy_all(moves, sem)

        def place(block, d):
            ylo, core = (a + block // 2) % 2, (c + block % 2) % 2
            return (ylo * 2 + core) * NZ + (z + d + NZ) % NZ

        for block in range(4):
            for i in range(nd):
                out[place(block, ds[i])] = done[block, i]
        for copy in copies:
            copy.wait()
        for block in range(4):
            half, total = block // 2, 0.0
            for k in range(nk):
                columns = slice(k * width, (k + 1) * width)
                if block % 2:
                    right = right_other[half, :, columns]
                else:
                    right = right_own[half, :, columns] if k < nk - 1 else far_own[half]
                total = total + dot_t(left[:, k * q : (k + 1) * q, :].reshape(nl * q, width), right)
            total = total.astype(jnp.bfloat16)
            for i in range(nl):
                out[place(block, ds[nd + i])] = total[i * q : (i + 1) * q]

    return pl.pallas_call(
        kernel,
        out_shape=vmem_out(4 * NZ, q, rows),
        in_specs=[VMEM] * 4 + [HBM] * (nl + 1),
        out_specs=VMEM,
        scratch_shapes=[
            pltpu.VMEM((nl, rows, width), jnp.bfloat16),
            pltpu.SemaphoreType.DMA((nl + 1,)),
        ],
        compiler_params=PARAMS,
        cost_estimate=cost(8 * nl * q * rows * nk * width, 2 * nl * rows * width),
        name="late",
    )(done, right_own, far_own, right_other, *lefts, *last)


def after(values, done):
    return lax.optimization_barrier((tuple(values), tuple(done)))[0]


def on_device(grads, lr_plan, ckpt_step):
    s, *quarters = scale(grads, lr_plan, ckpt_step)
    rows = s.shape[0]
    swap = lambda v: take_from(v, C, 2, 1)

    heads = [take_from(v, X, NX, dx) for v, dx in zip(quarters[1:], (1, -1, 2))]
    other = take_from(s, YL, 2, 1)
    ring = {0: jnp.concatenate([quarters[0]] + heads, axis=0)}
    ring[1], ring[-1] = take_from(ring[0], Z, NZ, 1), take_from(ring[0], Z, NZ, -1)
    (ready,) = after((s,), heads)
    fs, bs = take_from(ready, X, NX, 1), take_from(ready, X, NX, -1)

    (up,), (down,) = after((ring[1],), (fs,)), after((ring[-1],), (bs,))
    ring[2], ring[-2] = take_from(up, Z, NZ, 1), take_from(down, Z, NZ, -1)
    (f_ready,), (b_ready,) = after((other,), (fs,)), after((other,), (bs,))
    fo, bo = take_from(f_ready, X, NX, 1), take_from(b_ready, X, NX, -1)

    (up,), (down,) = after((ring[2],), (fo,)), after((ring[-2],), (bo,))
    ring[3], ring[-3] = take_from(up, Z, NZ, 1), take_from(down, Z, NZ, -1)
    (f_ready,), (b_ready,) = after((fs,), (fo,)), (bo,)
    far_s, far_o = take_from(f_ready, X, NX, 1), take_from(b_ready, X, NX, -1)

    first = [ring[d] for d in (0, 1, -1, 2, -2)]
    left, right_own, acc = own_products(first, [[s, fs, bs], [other, fo, bo]])
    half = rows // 2
    (down,) = (ring[-3],)
    last = (take_from(ring[3][:half], Z, NZ, 1), take_from(down[half:], Z, NZ, -1))

    ready = after((s,), (fs, bs)) + after((fs, bs, other), (acc,))
    ready += after((fo, bo, far_s, far_o), (ring[3], ring[-3]))
    swapped = [swap(v) for v in ready]
    right_other, far_own, done = all_products(
        left,
        acc,
        [swapped[:3] + swapped[6:7], swapped[3:6] + swapped[7:]],
        [far_s, far_o],
    )
    send = late_products(
        done, right_own, far_own, right_other, [ring[3], ring[-3]], last, (0, 1, -1, 2, -2, 3, -3, 4)
    )
    got = lax.all_to_all(send, (YL, C, YH, X), 0, 0)
    q = rows // NX
    got = got.reshape(2, 2, 2, NX, q, rows).astype(jnp.float32)
    total = got[:, :, 0] + got[:, :, 1]
    return total.reshape(2 * 2 * NX * q, rows).T


def solution(mesh):
    fine = Mesh(mesh.devices.reshape(NZ, 2, 2, 2, NX), (Z, YL, C, YH, X))
    spec = P((Z, YL, C), (YH, X))
    return jax.shard_map(
        on_device, mesh=fine, in_specs=(spec, P(), P()), out_specs=spec, check_vma=False
    )
```

```python
import jax
import jax.numpy as jnp
from jax import lax
from jax.experimental import pallas as pl
from jax.experimental.pallas import tpu as pltpu
from jax.sharding import Mesh, PartitionSpec as P

PROJ = 2048
CKPT = 4
FEATURES = 8192

Z, YL, C, YH, X = "z", "ylo", "core", "yhi", "x"
NZ, NX = 8, 4
SMEM = pl.BlockSpec(memory_space=pltpu.SMEM)
VMEM = pl.BlockSpec(memory_space=pltpu.VMEM)
HBM = pl.BlockSpec(memory_space=pltpu.HBM)


def take_from(value, axis, size, step):
    return lax.ppermute(value, axis, [(i, (i - step) % size) for i in range(size)])


def dot_t(left, right):
    return lax.dot_general(left, right, (((1,), (1,)), ((), ())), preferred_element_type=jnp.float32)


def scale_kernel(plan_ref, step_ref, grads_ref, out_ref, *quarter_refs):
    x = lax.axis_index(X)
    mine = ((lax.axis_index(YH) * NX + x) * grads_ref.shape[1]) // PROJ
    rate = [plan_ref[step_ref[i]] for i in range(CKPT)]
    own = plan_ref[step_ref[mine]]
    whole = rate[0] + rate[1] + rate[2] + rate[3]
    shape = (8, grads_ref.shape[1])
    weight = jnp.full(shape, own, jnp.float32) / jnp.full(shape, whole, jnp.float32)
    weight = weight * (CKPT / jnp.sqrt(jnp.full(shape, FEATURES, jnp.float32)))
    factor = jnp.sqrt(weight)[:1]
    out_ref[...] = (grads_ref[...].astype(jnp.float32) * factor).astype(jnp.bfloat16)
    for ref, dx in zip(quarter_refs, (0, 1, -1, 2)):
        q = ref.shape[0]
        first = pl.multiple_of(((x - dx + NX) % NX) * q, q)
        ref[...] = out_ref[pl.ds(first, q), :]


def scale(grads, lr_plan, ckpt_step):
    rows, width = grads.shape
    quarter = jax.ShapeDtypeStruct((rows // NX, width), jnp.bfloat16)
    return pl.pallas_call(
        scale_kernel,
        out_shape=[jax.ShapeDtypeStruct((rows, width), jnp.bfloat16)] + [quarter] * NX,
        in_specs=[SMEM, SMEM, VMEM],
        out_specs=[VMEM] * (1 + NX),
        name="scale",
    )(lr_plan, ckpt_step, grads)


def copy_all(moves, sem):
    copies = [pltpu.make_async_copy(src, dst, sem.at[i]) for i, (src, dst) in enumerate(moves)]
    for copy in copies:
        copy.start()
    return copies


def cost(flops, bytes_accessed):
    return pl.CostEstimate(flops=flops, bytes_accessed=bytes_accessed, transcendentals=0)


def vmem_out(*shape, dtype=jnp.bfloat16):
    return jax.ShapeDtypeStruct(shape, dtype)


PARAMS = pltpu.CompilerParams(vmem_limit_bytes=16 * 2**20)


def own_products(lefts, rights):
    rows, width = lefts[0].shape
    q, nd, nk = rows // NX, len(lefts), len(rights[0])

    def kernel(*refs):
        left_in, right_in = refs[:nd], refs[nd : nd + 2 * nk]
        left, right, acc, sem = refs[nd + 2 * nk :]
        moves = [(left_in[i], left.at[i]) for i in range(nd)]
        moves += [
            (right_in[i], right.at[i // nk, :, pl.ds(i % nk * width, width)]) for i in range(2 * nk)
        ]
        copies = copy_all(moves, sem)
        for copy in copies[:nd]:
            copy.wait()
        for half in range(2):
            total = 0.0
            for k in range(nk):
                copies[nd + half * nk + k].wait()
                part = left[:, k * q : (k + 1) * q, :].reshape(nd * q, width)
                total = total + dot_t(part, right[half, :, k * width : (k + 1) * width])
            acc[half] = total

    return pl.pallas_call(
        kernel,
        out_shape=[
            vmem_out(nd, rows, width),
            vmem_out(2, rows, nk * width),
            vmem_out(2, nd * q, rows, dtype=jnp.float32),
        ],
        in_specs=[HBM] * (nd + 2 * nk),
        out_specs=[VMEM] * 3,
        scratch_shapes=[pltpu.SemaphoreType.DMA((nd + 2 * nk,))],
        compiler_params=PARAMS,
        cost_estimate=cost(4 * nd * q * rows * nk * width, 2 * (nd + 2 * nk) * rows * width),
        name="own",
    )(*lefts, *rights[0], *rights[1])


def all_products(left, acc, rights, fars):
    nd, rows, width = left.shape
    q, nk = rows // NX, len(rights[0])

    def kernel(left, acc, *refs):
        right_in, far_in = refs[: 2 * nk], refs[2 * nk : 2 * nk + 2]
        right, far, out, sem = refs[2 * nk + 2 :]
        moves = [
            (right_in[i], right.at[i // nk, :, pl.ds(i % nk * width, width)]) for i in range(2 * nk)
        ]
        moves += [(far_in[i], far.at[i]) for i in range(2)]
        copies = copy_all(moves, sem)

        def part(k):
            return left[:, k * q : (k + 1) * q, :].reshape(nd * q, width)

        for half in range(2):
            total = 0.0
            for k in range(nk):
                copies[half * nk + k].wait()
                total = total + dot_t(part(k), right[half, :, k * width : (k + 1) * width])
            out[2 * half + 1] = total.astype(jnp.bfloat16).reshape(nd, q, rows)
        for half in range(2):
            copies[2 * nk + half].wait()
            total = acc[half] + dot_t(part(nk - 1), far[half])
            out[2 * half] = total.astype(jnp.bfloat16).reshape(nd, q, rows)

    return pl.pallas_call(
        kernel,
        out_shape=[
            vmem_out(2, rows, nk * width),
            vmem_out(2, rows, width),
            vmem_out(4, nd, q, rows),
        ],
        in_specs=[VMEM, VMEM] + [HBM] * (2 * nk + 2),
        out_specs=[VMEM] * 3,
        scratch_shapes=[pltpu.SemaphoreType.DMA((2 * nk + 2,))],
        compiler_params=PARAMS,
        cost_estimate=cost(4 * nd * q * rows * (nk + 1) * width, 4 * (nk + 1) * rows * width),
        name="rest",
    )(left, acc, *rights[0], *rights[1], *fars)


def late_products(done, right_own, far_own, right_other, lefts, last, ds):
    nd, q, rows = done.shape[1:]
    width = far_own.shape[2]
    nl, cut, nk = len(lefts) + 1, last[0].shape[0], NX

    def kernel(done, right_own, far_own, right_other, *refs):
        left_in, out, left, sem = refs[: nl + 1], refs[-3], refs[-2], refs[-1]
        z, a, c = (lax.axis_index(n) for n in (Z, YL, C))
        moves = [(left_in[i], left.at[i]) for i in range(nl - 1)]
        moves += [
            (left_in[nl - 1], left.at[nl - 1, pl.ds(0, cut)]),
            (left_in[nl], left.at[nl - 1, pl.ds(cut, rows - cut)]),
        ]
        copies = copy_all(moves, sem)

        def place(block, d):
            ylo, core = (a + block // 2) % 2, (c + block % 2) % 2
            return (ylo * 2 + core) * NZ + (z + d + NZ) % NZ

        for block in range(4):
            for i in range(nd):
                out[place(block, ds[i])] = done[block, i]
        for copy in copies:
            copy.wait()
        for block in range(4):
            half, total = block // 2, 0.0
            for k in range(nk):
                columns = slice(k * width, (k + 1) * width)
                if block % 2:
                    right = right_other[half, :, columns]
                else:
                    right = right_own[half, :, columns] if k < nk - 1 else far_own[half]
                total = total + dot_t(left[:, k * q : (k + 1) * q, :].reshape(nl * q, width), right)
            total = total.astype(jnp.bfloat16)
            for i in range(nl):
                out[place(block, ds[nd + i])] = total[i * q : (i + 1) * q]

    return pl.pallas_call(
        kernel,
        out_shape=vmem_out(4 * NZ, q, rows),
        in_specs=[VMEM] * 4 + [HBM] * (nl + 1),
        out_specs=VMEM,
        scratch_shapes=[
            pltpu.VMEM((nl, rows, width), jnp.bfloat16),
            pltpu.SemaphoreType.DMA((nl + 1,)),
        ],
        compiler_params=PARAMS,
        cost_estimate=cost(8 * nl * q * rows * nk * width, 2 * nl * rows * width),
        name="late",
    )(done, right_own, far_own, right_other, *lefts, *last)


def after(values, done):
    return lax.optimization_barrier((tuple(values), tuple(done)))[0]


def on_device(grads, lr_plan, ckpt_step):
    s, *quarters = scale(grads, lr_plan, ckpt_step)
    rows = s.shape[0]
    swap = lambda v: take_from(v, C, 2, 1)

    heads = [take_from(v, X, NX, dx) for v, dx in zip(quarters[1:], (1, -1, 2))]
    other = take_from(s, YL, 2, 1)
    ring = {0: jnp.concatenate([quarters[0]] + heads, axis=0)}
    ring[1], ring[-1] = take_from(ring[0], Z, NZ, 1), take_from(ring[0], Z, NZ, -1)
    (ready,) = after((s,), heads)
    fs, bs = take_from(ready, X, NX, 1), take_from(ready, X, NX, -1)

    (up,), (down,) = after((ring[1],), (fs,)), after((ring[-1],), (bs,))
    ring[2], ring[-2] = take_from(up, Z, NZ, 1), take_from(down, Z, NZ, -1)
    (f_ready,), (b_ready,) = after((other,), (fs,)), after((other,), (bs,))
    fo, bo = take_from(f_ready, X, NX, 1), take_from(b_ready, X, NX, -1)

    (up,), (down,) = after((ring[2],), (fo,)), after((ring[-2],), (bo,))
    ring[3], ring[-3] = take_from(up, Z, NZ, 1), take_from(down, Z, NZ, -1)
    (f_ready,), (b_ready,) = after((fs,), (fo,)), (bo,)
    far_s, far_o = take_from(f_ready, X, NX, 1), take_from(b_ready, X, NX, -1)

    first = [ring[d] for d in (0, 1, -1, 2, -2)]
    left, right_own, acc = own_products(first, [[s, fs, bs], [other, fo, bo]])
    cut = rows * 6 // 16
    (down,) = (ring[-3],)
    last = (take_from(ring[3][:cut], Z, NZ, 1), take_from(down[cut:], Z, NZ, -1))

    ready = after((s,), (fs, bs)) + after((fs, bs, other), (acc,))
    ready += after((fo, bo, far_s, far_o), (ring[3], ring[-3]))
    swapped = [swap(v) for v in ready]
    right_other, far_own, done = all_products(
        left,
        acc,
        [swapped[:3] + swapped[6:7], swapped[3:6] + swapped[7:]],
        [far_s, far_o],
    )
    send = late_products(
        done, right_own, far_own, right_other, [ring[3], ring[-3]], last, (0, 1, -1, 2, -2, 3, -3, 4)
    )
    got = lax.all_to_all(send, (YL, C, YH, X), 0, 0)
    q = rows // NX
    got = got.reshape(2, 2, 2, NX, q, rows).astype(jnp.float32)
    total = got[:, :, 0] + got[:, :, 1]
    return total.reshape(2 * 2 * NX * q, rows).T


def solution(mesh):
    fine = Mesh(mesh.devices.reshape(NZ, 2, 2, 2, NX), (Z, YL, C, YH, X))
    spec = P((Z, YL, C), (YH, X))
    return jax.shard_map(
        on_device, mesh=fine, in_specs=(spec, P(), P()), out_specs=spec, check_vma=False
    )
```
